32 devices in a mesh: var: 8 (over z, core), tp: 4 (over y, x).
Axes of the slice: x: 2, y: 2, z: 4, core: 2. Of those that a mesh axis runs over, the one named last changes fastest.
Arguments:
- hidden_in: bfloat16 [24, 384, 2048], P('var'), may hold values from -100 to 100
- run_table: int32 [24, 2], P('var'), may hold values 0 or 1
- qkv_weight: bfloat16 [2048, 3072], P('var', 'tp'), may hold values from -1 to 1
- out_weight: bfloat16 [2048, 2048], P('tp', 'var'), may hold values from -0.125 to 0.125
- gate_up_weight: bfloat16 [2048, 2, 8192], P('var', None, 'tp'), may hold values from -0.125 to 0.125
- down_weight: bfloat16 [8192, 2048], P('tp', 'var'), may hold values from -0.0625 to 0.0625
Outputs:
- layer_out: bfloat16 [24, 384, 2048], P('var')
The draws below stay inside these ranges and needn't reach their ends.
All inputs are finite; a program needn't handle non-finite values. No bound on the sum of `run_table` on one device may be relied on, other than what follows from the above.
Results may differ from the reference program's by a relative error of at most 0.0075.
Values may be sent and summed in bfloat16 or wider, within the bound.
A program may use at most 128 MiB of HBM per device.

```python
import jax
import jax.numpy as jnp
from jax import lax

D = 2048
FF = 8192
QUERY_HEADS = 32
KEY_VALUE_HEADS = 8
HEAD_SIZE = 64
PROMPT_LENGTH = 384
SEQS = 24
N_TP = 4


def draw_hidden_in(key, part):
    key_collection = jax.random.split(jax.random.fold_in(key, 11), 3)
    full_shape = (SEQS, PROMPT_LENGTH, D)
    base_field = jax.random.normal(key_collection[0], full_shape, jnp.float32)
    row_scale = jnp.exp(jax.random.uniform(key_collection[1], (SEQS, PROMPT_LENGTH, 1), jnp.float32, jnp.log(0.3), jnp.log(3.0)))
    col_scale = jnp.exp(jax.random.uniform(key_collection[2], (1, 1, D), jnp.float32, jnp.log(0.3), jnp.log(3.0)))
    drawn = base_field * row_scale * col_scale
    return jnp.clip(drawn, -100.0, 100.0).astype(jnp.bfloat16)


def draw_qkv_weight(key, part):
    key_collection = jax.random.split(jax.random.fold_in(key, 23), 1)
    query_slice = QUERY_HEADS // N_TP
    key_value_slice = KEY_VALUE_HEADS // N_TP
    block_width = (query_slice + 2 * key_value_slice) * HEAD_SIZE
    column_count = N_TP * block_width
    base_field = jax.random.normal(key_collection[0], (D, column_count), jnp.float32) * D ** (-0.5)
    return jnp.clip(base_field, -1.0, 1.0).astype(jnp.bfloat16)


def set_ends(result, own_key, least, top_value):
    longest = result.shape.index(max(result.shape))
    spots = []
    for shift in (0, 1):
        where = [jax.random.randint(jax.random.fold_in(own_key, axis), (), 0, length) for axis, length in enumerate(result.shape)]
        where[longest] = (where[longest] + shift) % result.shape[longest]
        spots.append(tuple(where))
    return result.at[spots[0]].set(least).at[spots[1]].set(top_value)


def level_of(key, shape, shards, least, high):
    factor_of, own = 1.0, jax.random.fold_in(key, 6)
    for position, parts in shards:
        heights = jnp.exp(jax.random.uniform(jax.random.fold_in(own, position), (parts,), jnp.float32, least / len(shards), high / len(shards)))
        factor_of = factor_of * jnp.repeat(heights, shape[position] // parts).reshape([-1 if axis == position else 1 for axis in range(len(shape))])
    return factor_of


def gaussian(own_key, dims, spread, most, cuts=(), kind=jnp.bfloat16):
    entries = jax.random.normal(own_key, dims, jnp.float32) * spread
    if len(cuts) > 0:
        entries = level_of(own_key, dims, cuts, -0.22, 0.18) * entries
    return jnp.clip(entries, min=-most, max=most).astype(kind)


def setup_inputs(seed: int = 0) -> dict:
    splits = jax.random.split(jax.random.key(seed), 7)
    hidden_in = draw_hidden_in(jax.random.fold_in(splits[6], 71), 0)
    run_table = set_ends((jax.random.randint(splits[1], (SEQS, 2), 0, 4) < 3).astype(jnp.int32), jax.random.fold_in(splits[1], 1), 0, 1)
    qkv_weight = draw_qkv_weight(jax.random.fold_in(splits[6], 71), 0)
    out_weight = gaussian(splits[3], (QUERY_HEADS * HEAD_SIZE, D), (QUERY_HEADS * HEAD_SIZE) ** -0.5, 0.125, ((0, 4), (1, 8)))
    gate_up_weight = gaussian(splits[4], (D, 2, FF), D ** -0.5, 0.125, ((0, 8), (2, 4)))
    down_weight = gaussian(splits[5], (FF, D), FF ** -0.5, 0.0625, ((0, 4), (1, 8)))
    return {"hidden_in": hidden_in, "run_table": run_table, "qkv_weight": qkv_weight, "out_weight": out_weight, "gate_up_weight": gate_up_weight, "down_weight": down_weight}


def rms_norm(tensor):
    widened = tensor.astype(jnp.float32)
    scaled = widened * lax.rsqrt(lax.optimization_barrier(jnp.mean(widened * widened, axis=-1, keepdims=True)) + 1e-05)
    return scaled.astype(jnp.bfloat16)

def rotary_embedding(tensor, token_positions):
    half_width = tensor.shape[-1] // 2
    exponent = jnp.arange(half_width, dtype=jnp.float32) * (2.0 / tensor.shape[-1])
    frequency = jnp.power(jnp.float32(500000.0), -exponent)
    angles = token_positions[:, None, None] * frequency[None, None, :]
    cosine = jnp.cos(angles)
    sine_part = jnp.sin(angles)
    first_half = tensor[..., :half_width]
    second_half = tensor[..., half_width:]
    return jnp.concatenate([first_half * cosine - second_half * sine_part, second_half * cosine + first_half * sine_part], axis=-1)

def block_sum(terms):
    rounded = lax.optimization_barrier(terms.astype(jnp.bfloat16))
    return lax.optimization_barrier(jnp.sum(rounded.astype(jnp.float32), axis=0))

def reference(hidden_in, run_table, qkv_weight, out_weight, gate_up_weight, down_weight):
    query_slice = QUERY_HEADS // N_TP
    key_value_slice = KEY_VALUE_HEADS // N_TP
    group_width = QUERY_HEADS // KEY_VALUE_HEADS
    ff_local = FF // N_TP
    out_blocks = out_weight.astype(jnp.float32).reshape(N_TP, query_slice * HEAD_SIZE, D)
    down_blocks = down_weight.astype(jnp.float32).reshape(N_TP, ff_local, D)
    gate_up_flat = gate_up_weight.reshape(D, 2 * FF)

    def one_sequence(packed):
        sequence, switches = packed
        switches = switches.astype(jnp.float32)
        normed = rms_norm(sequence)
        projected_rows = jnp.dot(normed, qkv_weight, preferred_element_type=jnp.float32)
        projected_rows = projected_rows.reshape(PROMPT_LENGTH, N_TP, query_slice + 2 * key_value_slice, HEAD_SIZE)
        token_positions = jnp.arange(PROMPT_LENGTH, dtype=jnp.float32)
        query_rows = rotary_embedding(projected_rows[:, :, :query_slice].reshape(PROMPT_LENGTH, QUERY_HEADS, HEAD_SIZE), token_positions).astype(jnp.bfloat16)
        keys_bfloat = rotary_embedding(projected_rows[:, :, query_slice:query_slice + key_value_slice].reshape(PROMPT_LENGTH, KEY_VALUE_HEADS, HEAD_SIZE), token_positions).astype(jnp.bfloat16)
        values_bfloat = projected_rows[:, :, query_slice + key_value_slice:].reshape(PROMPT_LENGTH, KEY_VALUE_HEADS, HEAD_SIZE).astype(jnp.bfloat16)
        grouped_queries = query_rows.reshape(PROMPT_LENGTH, KEY_VALUE_HEADS, group_width, HEAD_SIZE).astype(jnp.float32)
        scores = jnp.einsum('qkgd,pkd->kgqp', grouped_queries, keys_bfloat.astype(jnp.float32)) * HEAD_SIZE ** (-0.5)
        causal = jnp.arange(PROMPT_LENGTH)[:, None] >= jnp.arange(PROMPT_LENGTH)[None, :]
        scores = jnp.where(causal, scores, jnp.float32(-1e+30))
        row_max = lax.optimization_barrier(jnp.max(scores, axis=-1, keepdims=True))
        exped = jnp.exp(scores - row_max)
        weights_bf = (exped / lax.optimization_barrier(jnp.sum(exped, axis=-1, keepdims=True))).astype(jnp.bfloat16)
        head_outputs = jnp.einsum('kgqp,pkd->qkgd', weights_bf.astype(jnp.float32), values_bfloat.astype(jnp.float32))
        head_outputs = head_outputs.astype(jnp.bfloat16).reshape(PROMPT_LENGTH, N_TP, query_slice * HEAD_SIZE)
        attn_terms = jnp.einsum('sjc,jcd->jsd', head_outputs.astype(jnp.float32), out_blocks)
        attention = block_sum(attn_terms)
        after_attention = (sequence.astype(jnp.float32) + switches[0] * attention).astype(jnp.bfloat16)
        normed_two = rms_norm(after_attention)
        gate_and_up = jnp.dot(normed_two, gate_up_flat, preferred_element_type=jnp.float32)
        hidden = (jax.nn.silu(gate_and_up[:, :FF]) * gate_and_up[:, FF:]).astype(jnp.bfloat16)
        mlp_terms = jnp.einsum('sjc,jcd->jsd', hidden.reshape(PROMPT_LENGTH, N_TP, ff_local).astype(jnp.float32), down_blocks)
        mlp = block_sum(mlp_terms)
        return (after_attention.astype(jnp.float32) + switches[1] * mlp).astype(jnp.bfloat16)
    return lax.map(one_sequence, (hidden_in, run_table))
```

```python
import jax
import jax.numpy as jnp
from jax import lax
from jax.sharding import PartitionSpec as P

QUERY_HEADS = 32
KEY_VALUE_HEADS = 8
HEAD_SIZE = 64
CORES = 2


def rms_norm(tensor):
    widened = tensor.astype(jnp.float32)
    scaled = widened * lax.rsqrt(jnp.mean(widened * widened, axis=-1, keepdims=True) + 1e-05)
    return scaled.astype(jnp.bfloat16)


def rotary_embedding(tensor, token_positions):
    half_width = tensor.shape[-1] // 2
    exponent = jnp.arange(half_width, dtype=jnp.float32) * (2.0 / tensor.shape[-1])
    frequency = jnp.power(jnp.float32(500000.0), -exponent)
    angles = token_positions[:, None, None] * frequency[None, None, :]
    cosine = jnp.cos(angles)
    sine_part = jnp.sin(angles)
    first_half = tensor[..., :half_width]
    second_half = tensor[..., half_width:]
    return jnp.concatenate(
        [
            first_half * cosine - second_half * sine_part,
            second_half * cosine + first_half * sine_part,
        ],
        axis=-1,
    )


def attend(query_rows, keys_bfloat, values_bfloat, score_scale):
    scores = (
        jnp.einsum("bqkgd,bpkd->bkgqp", query_rows, keys_bfloat, preferred_element_type=jnp.float32)
        * score_scale
    )
    length = scores.shape[-1]
    causal = jnp.arange(length)[:, None] >= jnp.arange(length)[None, :]
    scores = jnp.where(causal, scores, jnp.float32(-1e30))
    row_max = jnp.max(scores, axis=-1, keepdims=True)
    exped = jnp.exp(scores - row_max)
    weights_bf = (exped / jnp.sum(exped, axis=-1, keepdims=True)).astype(jnp.bfloat16)
    head_outputs = jnp.einsum(
        "bkgqp,bpkd->bqkgd", weights_bf, values_bfloat, preferred_element_type=jnp.float32
    )
    return head_outputs.astype(jnp.bfloat16)


def after(tensor, earlier):
    return lax.optimization_barrier((tensor, earlier))[0]


def ring(shard, earlier):
    var_count = lax.axis_size("var")
    forward = [(i, (i + CORES) % var_count) for i in range(var_count)]
    if earlier is not None:
        shard = after(shard, earlier)
    held = [shard]
    for _ in range(var_count // CORES - 1):
        held.append(lax.ppermute(held[-1], "var", forward))
    return held


def swap(held):
    var_count = lax.axis_size("var")
    pairs = [(i, i + 1 - 2 * (i % CORES)) for i in range(var_count)]
    return [lax.ppermute(shard, "var", pairs) for shard in held]


def pairs_of(mine, other):
    return [block for pair in zip(mine, other) for block in pair]


def shards(hidden_in, run_table, qkv_weight, out_weight, gate_up_weight, down_weight):
    tensor_parallel_count = lax.axis_size("tp")
    var_count = lax.axis_size("var")
    seq_count, full_len, model_width = hidden_in.shape
    row_count = seq_count * full_len
    query_slice = QUERY_HEADS // tensor_parallel_count
    key_value_slice = KEY_VALUE_HEADS // tensor_parallel_count
    group_width = QUERY_HEADS // KEY_VALUE_HEADS
    switches = run_table.astype(jnp.float32)
    bf16 = jnp.bfloat16

    query_width = query_slice * HEAD_SIZE
    half_ff = down_weight.shape[0] // 2
    q_ring = ring(qkv_weight[:, :query_width], None)
    kv_ring = ring(qkv_weight[:, query_width:], None)
    out_ring = ring(out_weight, kv_ring[-1])
    gate_ring = ring(gate_up_weight[:, 0, :], q_ring[-1])
    up_ring = ring(gate_up_weight[:, 1, :], out_ring[-1])
    down_a_ring = ring(down_weight[:half_ff], gate_ring[-1])
    down_b_ring = ring(down_weight[half_ff:], up_ring[-1])

    q_weight = jnp.concatenate(pairs_of(q_ring, swap(q_ring)), axis=0)
    kv_weight = jnp.concatenate(pairs_of(kv_ring, swap(kv_ring)), axis=0)
    out_full = jnp.concatenate(pairs_of(out_ring, swap(out_ring)), axis=1)

    block = model_width // var_count
    me = lax.axis_index("var")
    chip, core = me // CORES, me % CORES
    chip_count = var_count // CORES
    order = []
    for step in range(chip_count):
        origin = (chip + chip_count - step) % chip_count
        order += [origin * CORES + core, origin * CORES + 1 - core]
    flat_in = hidden_in.reshape(row_count, model_width)
    ordered_in = jnp.concatenate(
        [lax.dynamic_slice_in_dim(flat_in, place * block, block, axis=1) for place in order], axis=1
    )

    columns = rms_norm(ordered_in)
    queries = jnp.dot(columns, q_weight, preferred_element_type=jnp.float32)
    keys_values = jnp.dot(columns, kv_weight, preferred_element_type=jnp.float32)
    queries = queries.reshape(seq_count, full_len, query_slice, HEAD_SIZE)
    keys_values = keys_values.reshape(seq_count, full_len, 2 * key_value_slice, HEAD_SIZE)
    token_positions = jnp.arange(full_len, dtype=jnp.float32)
    query_rows = rotary_embedding(queries, token_positions).astype(bf16)
    query_rows = query_rows.reshape(seq_count, full_len, key_value_slice, group_width, HEAD_SIZE)
    keys_bfloat = rotary_embedding(keys_values[:, :, :key_value_slice], token_positions).astype(bf16)
    values_bfloat = keys_values[:, :, key_value_slice:].astype(bf16)
    head_outputs = attend(query_rows, keys_bfloat, values_bfloat, HEAD_SIZE ** (-0.5))
    head_rows = head_outputs.reshape(row_count, query_width)
    attn_terms = jnp.dot(head_rows, out_full, preferred_element_type=jnp.float32)
    attention = lax.psum(attn_terms.astype(bf16), "tp").astype(jnp.float32)
    attn_switch = jnp.repeat(switches[:, 0], full_len)[:, None]
    whole_after = (ordered_in.astype(jnp.float32) + attn_switch * attention).astype(bf16)

    mlp_input = rms_norm(whole_after)
    gate_weight = jnp.concatenate(pairs_of(gate_ring, swap(gate_ring)), axis=0)
    up_weight = jnp.concatenate(pairs_of(up_ring, swap(up_ring)), axis=0)
    gate = jnp.dot(mlp_input, gate_weight, preferred_element_type=jnp.float32)
    up = jnp.dot(mlp_input, up_weight, preferred_element_type=jnp.float32)
    hidden = (jax.nn.silu(gate) * up).astype(bf16)

    mlp_switch = jnp.repeat(switches[:, 1], full_len)[:, None]
    down_a_swap, down_b_swap = swap(down_a_ring), swap(down_b_ring)
    layer_out = jnp.zeros((row_count, model_width), bf16)
    for step in range(chip_count):
        mine = jnp.concatenate([down_a_ring[step], down_b_ring[step]], axis=0)
        other = jnp.concatenate([down_a_swap[step], down_b_swap[step]], axis=0)
        down_pair = jnp.concatenate([mine, other], axis=1)
        terms = jnp.dot(hidden, down_pair, preferred_element_type=jnp.float32)
        terms = terms.astype(bf16)
        if step > 0:
            terms = after(terms, summed)
        summed = lax.psum(terms, "tp")
        mlp = summed.astype(jnp.float32)
        residual = whole_after[:, 2 * step * block : 2 * (step + 1) * block]
        result = (residual.astype(jnp.float32) + mlp_switch * mlp).astype(bf16)
        for half in range(2):
            layer_out = lax.dynamic_update_slice_in_dim(
                layer_out,
                result[:, half * block : (half + 1) * block],
                order[2 * step + half] * block,
                axis=1,
            )
    return layer_out.reshape(seq_count, full_len, model_width)


def solution(mesh):
    return jax.shard_map(
        shards,
        mesh=mesh,
        in_specs=(
            P("var", None, None),
            P("var", None),
            P("var", "tp"),
            P("tp", "var"),
            P("var", None, "tp"),
            P("tp", "var"),
        ),
        out_specs=P("var", None, None),
        check_vma=False,
    )
```

```python
import jax
import jax.numpy as jnp
from jax import lax
from jax.sharding import PartitionSpec as P

QUERY_HEADS = 32
KEY_VALUE_HEADS = 8
HEAD_SIZE = 64
CORES = 2


def rms_norm(tensor):
    widened = tensor.astype(jnp.float32)
    scaled = widened * lax.rsqrt(jnp.mean(widened * widened, axis=-1, keepdims=True) + 1e-05)
    return scaled.astype(jnp.bfloat16)


def rotary_embedding(tensor, token_positions):
    half_width = tensor.shape[-1] // 2
    exponent = jnp.arange(half_width, dtype=jnp.float32) * (2.0 / tensor.shape[-1])
    frequency = jnp.power(jnp.float32(500000.0), -exponent)
    angles = token_positions[:, None, None] * frequency[None, None, :]
    cosine = jnp.cos(angles)
    sine_part = jnp.sin(angles)
    first_half = tensor[..., :half_width]
    second_half = tensor[..., half_width:]
    return jnp.concatenate(
        [
            first_half * cosine - second_half * sine_part,
            second_half * cosine + first_half * sine_part,
        ],
        axis=-1,
    )


def attend(query_rows, keys_bfloat, values_bfloat, score_scale):
    scores = (
        jnp.einsum("bqkgd,bpkd->bkgqp", query_rows, keys_bfloat, preferred_element_type=jnp.float32)
        * score_scale
    )
    length = scores.shape[-1]
    causal = jnp.arange(length)[:, None] >= jnp.arange(length)[None, :]
    scores = jnp.where(causal, scores, jnp.float32(-1e30))
    row_max = jnp.max(scores, axis=-1, keepdims=True)
    exped = jnp.exp(scores - row_max)
    weights_bf = (exped / jnp.sum(exped, axis=-1, keepdims=True)).astype(jnp.bfloat16)
    head_outputs = jnp.einsum(
        "bkgqp,bpkd->bqkgd", weights_bf, values_bfloat, preferred_element_type=jnp.float32
    )
    return head_outputs.astype(jnp.bfloat16)


def after(tensor, earlier):
    return lax.optimization_barrier((tensor, earlier))[0]


def ring(shard, earlier):
    var_count = lax.axis_size("var")
    forward = [(i, (i + CORES) % var_count) for i in range(var_count)]
    if earlier is not None:
        shard = after(shard, earlier)
    held = [shard]
    for _ in range(var_count // CORES - 1):
        held.append(lax.ppermute(held[-1], "var", forward))
    return held


def swap(held):
    var_count = lax.axis_size("var")
    pairs = [(i, i + 1 - 2 * (i % CORES)) for i in range(var_count)]
    return [lax.ppermute(shard, "var", pairs) for shard in held]


def assemble(held, order, axis):
    block = held[0].shape[axis]
    shape = list(held[0].shape)
    shape[axis] = block * len(held)
    whole = jnp.zeros(tuple(shape), held[0].dtype)
    for shard, place in zip(held, order):
        whole = lax.dynamic_update_slice_in_dim(whole, shard, place * block, axis=axis)
    return whole


def partner(tensor, bit):
    pairs = [(i, i ^ (1 << bit)) for i in range(lax.axis_size("tp"))]
    return lax.ppermute(tensor, "tp", pairs)


def side(bit):
    return (lax.axis_index("tp") >> bit) & 1


def scatter_rows(terms, bits):
    start = 0
    for bit in bits:
        half = terms.shape[0] // 2
        mine = side(bit)
        sent = lax.dynamic_slice_in_dim(terms, (1 - mine) * half, half, axis=0)
        kept = lax.dynamic_slice_in_dim(terms, mine * half, half, axis=0)
        total = kept.astype(jnp.float32) + partner(sent, bit).astype(jnp.float32)
        terms = total.astype(jnp.bfloat16)
        start = start + mine * half
    return total, start


def gather_rows(rows, bits):
    for bit in bits[:0:-1]:
        half = rows.shape[0]
        mine = side(bit)
        joined = jnp.zeros((2 * half,) + rows.shape[1:], rows.dtype)
        joined = lax.dynamic_update_slice_in_dim(joined, rows, mine * half, axis=0)
        rows = lax.dynamic_update_slice_in_dim(joined, partner(rows, bit), (1 - mine) * half, axis=0)
    return rows, partner(rows, bits[0]), side(bits[0])


def shards(hidden_in, run_table, qkv_weight, out_weight, gate_up_weight, down_weight):
    tensor_parallel_count = lax.axis_size("tp")
    var_count = lax.axis_size("var")
    chip_count = var_count // CORES
    seq_count, full_len, model_width = hidden_in.shape
    row_count = seq_count * full_len
    query_slice = QUERY_HEADS // tensor_parallel_count
    key_value_slice = KEY_VALUE_HEADS // tensor_parallel_count
    group_width = QUERY_HEADS // KEY_VALUE_HEADS
    switches = run_table.astype(jnp.float32)
    bf16 = jnp.bfloat16

    query_width = query_slice * HEAD_SIZE
    half_ff = down_weight.shape[0] // 2
    q_ring = ring(qkv_weight[:, :query_width], None)
    kv_ring = ring(qkv_weight[:, query_width:], None)
    out_ring = ring(out_weight, kv_ring[-1])
    gate_ring = ring(gate_up_weight[:, 0, :], q_ring[-2])
    up_ring = ring(gate_up_weight[:, 1, :], out_ring[-2])
    down_a_ring = ring(down_weight[:half_ff], gate_ring[-2])
    down_b_ring = ring(down_weight[half_ff:], up_ring[-2])

    me = lax.axis_index("var")
    chip, core = me // CORES, me % CORES
    origins = [(chip + chip_count - step) % chip_count for step in range(chip_count)]
    order = [place for origin in origins for place in (origin * CORES + core, origin * CORES + 1 - core)]

    def whole(held, axis):
        return assemble([shard for pair in zip(held, swap(held)) for shard in pair], order, axis)

    columns = rms_norm(hidden_in).reshape(row_count, model_width)
    queries = jnp.dot(columns, whole(q_ring, 0), preferred_element_type=jnp.float32)
    keys_values = jnp.dot(columns, whole(kv_ring, 0), preferred_element_type=jnp.float32)
    queries = queries.reshape(seq_count, full_len, query_slice, HEAD_SIZE)
    keys_values = keys_values.reshape(seq_count, full_len, 2 * key_value_slice, HEAD_SIZE)
    token_positions = jnp.arange(full_len, dtype=jnp.float32)
    query_rows = rotary_embedding(queries, token_positions).astype(bf16)
    query_rows = query_rows.reshape(seq_count, full_len, key_value_slice, group_width, HEAD_SIZE)
    keys_bfloat = rotary_embedding(keys_values[:, :, :key_value_slice], token_positions).astype(bf16)
    values_bfloat = keys_values[:, :, key_value_slice:].astype(bf16)
    head_outputs = attend(query_rows, keys_bfloat, values_bfloat, HEAD_SIZE ** (-0.5))
    head_rows = head_outputs.reshape(row_count, query_width)
    attn_terms = jnp.dot(head_rows, whole(out_ring, 1), preferred_element_type=jnp.float32)
    attention = lax.psum(attn_terms.astype(bf16), "tp").astype(jnp.float32)
    attn_switch = jnp.repeat(switches[:, 0], full_len)[:, None]
    flat_in = hidden_in.reshape(row_count, model_width)
    whole_after = (flat_in.astype(jnp.float32) + attn_switch * attention).astype(bf16)

    mlp_input = rms_norm(whole_after)
    gate = jnp.dot(mlp_input, whole(gate_ring, 0), preferred_element_type=jnp.float32)
    up = jnp.dot(mlp_input, whole(up_ring, 0), preferred_element_type=jnp.float32)
    hidden = (jax.nn.silu(gate) * up).astype(bf16)

    mlp_switch = jnp.repeat(switches[:, 1], full_len)[:, None]
    down_a_swap, down_b_swap = swap(down_a_ring), swap(down_b_ring)
    width = model_width // chip_count
    forth = list(range(tensor_parallel_count.bit_length() - 1))
    early = chip_count // 2
    layer_out = jnp.zeros((row_count, model_width), bf16)
    for steps in [list(range(early))] + [[step] for step in range(early, chip_count)]:
        down_blocks = []
        for step in steps:
            pair = jnp.zeros((2 * half_ff, width), bf16)
            for tensor, row, place in (
                (down_a_ring, 0, core),
                (down_b_ring, half_ff, core),
                (down_a_swap, 0, 1 - core),
                (down_b_swap, half_ff, 1 - core),
            ):
                pair = lax.dynamic_update_slice(pair, tensor[step], (row, place * (width // CORES)))
            down_blocks.append(pair)
        terms = jnp.dot(
            hidden, jnp.concatenate(down_blocks, axis=1), preferred_element_type=jnp.float32
        ).astype(bf16)
        half_rows = row_count // 2
        for row, bits in ((0, forth), (half_rows, forth[::-1])):
            mlp, start = scatter_rows(terms[row : row + half_rows], bits)
            count = mlp.shape[0]
            residual = jnp.concatenate(
                [
                    lax.dynamic_slice(whole_after, (row + start, origins[step] * width), (count, width))
                    for step in steps
                ],
                axis=1,
            )
            switch = lax.dynamic_slice_in_dim(mlp_switch, row + start, count, axis=0)
            result = (residual.astype(jnp.float32) + switch * mlp).astype(bf16)
            near, far, first = gather_rows(result, bits)
            for part, lower in ((near, first), (far, 1 - first)):
                for number, step in enumerate(steps):
                    layer_out = lax.dynamic_update_slice(
                        layer_out,
                        part[:, number * width : (number + 1) * width],
                        (row + lower * part.shape[0], origins[step] * width),
                    )
    return layer_out.reshape(seq_count, full_len, model_width)


def solution(mesh):
    return jax.shard_map(
        shards,
        mesh=mesh,
        in_specs=(
            P("var", None, None),
            P("var", None),
            P("var", "tp"),
            P("tp", "var"),
            P("var", None, "tp"),
            P("tp", "var"),
        ),
        out_specs=P("var", None, None),
        check_vma=False,
    )
```

```python
import jax
import jax.numpy as jnp
from jax import lax
from jax.sharding import PartitionSpec as P

QUERY_HEADS = 32
KEY_VALUE_HEADS = 8
HEAD_SIZE = 64
CORES = 2


def rms_norm(tensor):
    widened = tensor.astype(jnp.float32)
    scaled = widened * lax.rsqrt(jnp.mean(widened * widened, axis=-1, keepdims=True) + 1e-05)
    return scaled.astype(jnp.bfloat16)


def rotary_embedding(tensor, token_positions):
    half_width = tensor.shape[-1] // 2
    exponent = jnp.arange(half_width, dtype=jnp.float32) * (2.0 / tensor.shape[-1])
    frequency = jnp.power(jnp.float32(500000.0), -exponent)
    angles = token_positions[:, None, None] * frequency[None, None, :]
    cosine = jnp.cos(angles)
    sine_part = jnp.sin(angles)
    first_half = tensor[..., :half_width]
    second_half = tensor[..., half_width:]
    return jnp.concatenate(
        [
            first_half * cosine - second_half * sine_part,
            second_half * cosine + first_half * sine_part,
        ],
        axis=-1,
    )


def attend(query_rows, keys_bfloat, values_bfloat, score_scale):
    scores = (
        jnp.einsum("bqkgd,bpkd->bkgqp", query_rows, keys_bfloat, preferred_element_type=jnp.float32)
        * score_scale
    )
    length = scores.shape[-1]
    causal = jnp.arange(length)[:, None] >= jnp.arange(length)[None, :]
    scores = jnp.where(causal, scores, jnp.float32(-1e30))
    row_max = jnp.max(scores, axis=-1, keepdims=True)
    exped = jnp.exp(scores - row_max)
    weights_bf = (exped / jnp.sum(exped, axis=-1, keepdims=True)).astype(jnp.bfloat16)
    head_outputs = jnp.einsum(
        "bkgqp,bpkd->bqkgd", weights_bf, values_bfloat, preferred_element_type=jnp.float32
    )
    return head_outputs.astype(jnp.bfloat16)


def after(tensor, earlier):
    return lax.optimization_barrier((tensor, earlier))[0]


def ring(shard, earlier=None, gates=()):
    var_count = lax.axis_size("var")
    forward = [(i, (i + CORES) % var_count) for i in range(var_count)]
    hops = var_count // CORES - 1
    held = [shard if earlier is None else after(shard, earlier)]
    for hop in range(hops):
        gate = hop - (hops - len(gates))
        sent = held[-1] if gate < 0 else after(held[-1], gates[gate])
        held.append(lax.ppermute(sent, "var", forward))
    return held


def swap(held):
    var_count = lax.axis_size("var")
    pairs = [(i, i + 1 - 2 * (i % CORES)) for i in range(var_count)]
    return [lax.ppermute(shard, "var", pairs) for shard in held]


def assemble(held, order, axis):
    block = held[0].shape[axis]
    shape = list(held[0].shape)
    shape[axis] = block * len(held)
    whole = jnp.zeros(tuple(shape), held[0].dtype)
    for shard, place in zip(held, order):
        whole = lax.dynamic_update_slice_in_dim(whole, shard, place * block, axis=axis)
    return whole


def partner(tensor, bit):
    pairs = [(i, i ^ (1 << bit)) for i in range(lax.axis_size("tp"))]
    return lax.ppermute(tensor, "tp", pairs)


def side(bit):
    return (lax.axis_index("tp") >> bit) & 1


def scatter_rows(terms, bits):
    start = 0
    for bit in bits:
        half = terms.shape[0] // 2
        mine = side(bit)
        sent = lax.dynamic_slice_in_dim(terms, (1 - mine) * half, half, axis=0)
        kept = lax.dynamic_slice_in_dim(terms, mine * half, half, axis=0)
        total = kept.astype(jnp.float32) + partner(sent, bit).astype(jnp.float32)
        terms = total.astype(jnp.bfloat16)
        start = start + mine * half
    return total, start


def gather_rows(rows, bits):
    for bit in bits[::-1]:
        other = partner(rows, bit)
        lower = side(bit) == 0
        rows = jnp.concatenate([jnp.where(lower, rows, other), jnp.where(lower, other, rows)], axis=0)
    return rows


def add_sum(terms, base, switch, bits):
    total, start = scatter_rows(terms, bits)
    count = total.shape[0]
    own = lax.dynamic_slice_in_dim(base, start, count, axis=0).astype(jnp.float32)
    own_switch = lax.dynamic_slice_in_dim(switch, start, count, axis=0)
    return gather_rows((own + own_switch * total).astype(jnp.bfloat16), bits)


def shards(hidden_in, run_table, qkv_weight, out_weight, gate_up_weight, down_weight):
    tensor_parallel_count = lax.axis_size("tp")
    var_count = lax.axis_size("var")
    chip_count = var_count // CORES
    seq_count, full_len, model_width = hidden_in.shape
    row_count = seq_count * full_len
    query_slice = QUERY_HEADS // tensor_parallel_count
    key_value_slice = KEY_VALUE_HEADS // tensor_parallel_count
    group_width = QUERY_HEADS // KEY_VALUE_HEADS
    switches = run_table.astype(jnp.float32)
    bf16 = jnp.bfloat16

    query_width = query_slice * HEAD_SIZE
    q_ring = ring(qkv_weight[:, :query_width])
    kv_ring = ring(qkv_weight[:, query_width:])
    out_ring = ring(out_weight, kv_ring[-2])
    gate_ring = ring(gate_up_weight[:, 0, :], q_ring[-2])
    up_ring = ring(gate_up_weight[:, 1, :], kv_ring[-1])

    me = lax.axis_index("var")
    chip, core = me // CORES, me % CORES
    origins = [(chip + chip_count - step) % chip_count for step in range(chip_count)]
    order = [place for origin in origins for place in (origin * CORES + core, origin * CORES + 1 - core)]

    def whole(held, axis):
        return assemble([shard for pair in zip(held, swap(held)) for shard in pair], order, axis)

    columns = rms_norm(hidden_in).reshape(row_count, model_width)
    queries = jnp.dot(columns, whole(q_ring, 0), preferred_element_type=jnp.float32)
    keys_values = jnp.dot(columns, whole(kv_ring, 0), preferred_element_type=jnp.float32)
    queries = queries.reshape(seq_count, full_len, query_slice, HEAD_SIZE)
    keys_values = keys_values.reshape(seq_count, full_len, 2 * key_value_slice, HEAD_SIZE)
    token_positions = jnp.arange(full_len, dtype=jnp.float32)
    query_rows = rotary_embedding(queries, token_positions).astype(bf16)
    query_rows = query_rows.reshape(seq_count, full_len, key_value_slice, group_width, HEAD_SIZE)
    keys_bfloat = rotary_embedding(keys_values[:, :, :key_value_slice], token_positions).astype(bf16)
    values_bfloat = keys_values[:, :, key_value_slice:].astype(bf16)
    head_outputs = attend(query_rows, keys_bfloat, values_bfloat, HEAD_SIZE ** (-0.5))
    head_rows = head_outputs.reshape(row_count, query_width)
    attn_terms = jnp.dot(head_rows, whole(out_ring, 1), preferred_element_type=jnp.float32).astype(bf16)
    attn_switch = jnp.repeat(switches[:, 0], full_len)[:, None]
    flat_in = hidden_in.reshape(row_count, model_width)
    forth = list(range(tensor_parallel_count.bit_length() - 1))
    half_width = model_width // 2
    whole_after = jnp.concatenate(
        [
            add_sum(attn_terms[:, :half_width], flat_in[:, :half_width], attn_switch, forth),
            add_sum(attn_terms[:, half_width:], flat_in[:, half_width:], attn_switch, forth[::-1]),
        ],
        axis=1,
    )

    mlp_input = rms_norm(whole_after)
    gate = jnp.dot(mlp_input, whole(gate_ring, 0), preferred_element_type=jnp.float32)
    up = jnp.dot(mlp_input, whole(up_ring, 0), preferred_element_type=jnp.float32)
    hidden = (jax.nn.silu(gate) * up).astype(bf16)

    half_ff = down_weight.shape[0] // 2
    gates = (whole_after, gate)
    down_a_ring = ring(down_weight[:half_ff], gate_ring[-2], gates)
    down_b_ring = ring(down_weight[half_ff:], up_ring[-2], gates)
    down_a_swap, down_b_swap = swap(down_a_ring), swap(down_b_ring)
    mlp_switch = jnp.repeat(switches[:, 1], full_len)[:, None]
    width = model_width // chip_count
    half_rows = row_count // 2
    early = chip_count // 2
    first_core = core == 0
    layer_out = jnp.zeros((row_count, model_width), bf16)
    for steps in (range(early), range(early, chip_count)):
        down_blocks = []
        for step in steps:
            mine = jnp.concatenate([down_a_ring[step], down_b_ring[step]], axis=0)
            other = jnp.concatenate([down_a_swap[step], down_b_swap[step]], axis=0)
            down_blocks += [jnp.where(first_core, mine, other), jnp.where(first_core, other, mine)]
        down_blocks = jnp.concatenate(down_blocks, axis=1)
        terms = jnp.dot(hidden, down_blocks, preferred_element_type=jnp.float32).astype(bf16)
        base = jnp.concatenate(
            [
                lax.dynamic_slice_in_dim(whole_after, origins[step] * width, width, axis=1)
                for step in steps
            ],
            axis=1,
        )
        result = jnp.concatenate(
            [
                add_sum(terms[:half_rows], base[:half_rows], mlp_switch[:half_rows], forth),
                add_sum(terms[half_rows:], base[half_rows:], mlp_switch[half_rows:], forth[::-1]),
            ],
            axis=0,
        )
        for number, step in enumerate(steps):
            layer_out = lax.dynamic_update_slice_in_dim(
                layer_out,
                result[:, number * width : (number + 1) * width],
                origins[step] * width,
                axis=1,
            )
    return layer_out.reshape(seq_count, full_len, model_width)


def solution(mesh):
    return jax.shard_map(
        shards,
        mesh=mesh,
        in_specs=(
            P("var", None, None),
            P("var", None),
            P("var", "tp"),
            P("tp", "var"),
            P("var", None, "tp"),
            P("tp", "var"),
        ),
        out_specs=P("var", None, None),
        check_vma=False,
    )
```

```python
import jax
import jax.numpy as jnp
from jax import lax
from jax.sharding import PartitionSpec as P

QUERY_HEADS = 32
KEY_VALUE_HEADS = 8
HEAD_SIZE = 64


def rms_norm(tensor):
    widened = tensor.astype(jnp.float32)
    scaled = widened * lax.rsqrt(jnp.mean(widened * widened, axis=-1, keepdims=True) + 1e-05)
    return scaled.astype(jnp.bfloat16)


def rotary_embedding(tensor, token_positions):
    half_width = tensor.shape[-1] // 2
    exponent = jnp.arange(half_width, dtype=jnp.float32) * (2.0 / tensor.shape[-1])
    frequency = jnp.power(jnp.float32(500000.0), -exponent)
    angles = token_positions[:, None, None] * frequency[None, None, :]
    cosine = jnp.cos(angles)
    sine_part = jnp.sin(angles)
    first_half = tensor[..., :half_width]
    second_half = tensor[..., half_width:]
    return jnp.concatenate(
        [
            first_half * cosine - second_half * sine_part,
            second_half * cosine + first_half * sine_part,
        ],
        axis=-1,
    )


def attend(query_rows, keys_bfloat, values_bfloat, score_scale):
    scores = (
        jnp.einsum("bqkgd,bpkd->bkgqp", query_rows, keys_bfloat, preferred_element_type=jnp.float32)
        * score_scale
    )
    length = scores.shape[-1]
    causal = jnp.arange(length)[:, None] >= jnp.arange(length)[None, :]
    scores = jnp.where(causal, scores, jnp.float32(-1e30))
    row_max = jnp.max(scores, axis=-1, keepdims=True)
    exped = jnp.exp(scores - row_max)
    weights_bf = (exped / jnp.sum(exped, axis=-1, keepdims=True)).astype(jnp.bfloat16)
    head_outputs = jnp.einsum(
        "bkgqp,bpkd->bqkgd", weights_bf, values_bfloat, preferred_element_type=jnp.float32
    )
    return head_outputs.astype(jnp.bfloat16)


def after(tensor, earlier):
    return lax.optimization_barrier((tensor, earlier))[0]


def gather(shard, axis, *earlier):
    shard = after(shard, earlier) if earlier else shard
    return lax.all_gather(shard, "var", axis=axis, tiled=True)


def partner(tensor, bit):
    pairs = [(i, i ^ (1 << bit)) for i in range(lax.axis_size("tp"))]
    return lax.ppermute(tensor, "tp", pairs)


def side(bit):
    return (lax.axis_index("tp") >> bit) & 1


def scatter_rows(terms, bits):
    start = 0
    for bit in bits:
        half = terms.shape[0] // 2
        mine = side(bit)
        sent = lax.dynamic_slice_in_dim(terms, (1 - mine) * half, half, axis=0)
        kept = lax.dynamic_slice_in_dim(terms, mine * half, half, axis=0)
        total = kept.astype(jnp.float32) + partner(sent, bit).astype(jnp.float32)
        terms = total.astype(jnp.bfloat16)
        start = start + mine * half
    return total, start


def gather_rows(rows, bits):
    for bit in bits[::-1]:
        other = partner(rows, bit)
        lower = side(bit) == 0
        rows = jnp.concatenate([jnp.where(lower, rows, other), jnp.where(lower, other, rows)], axis=0)
    return rows


def add_sum(terms, base, switch, bits):
    total, start = scatter_rows(terms, bits)
    count = total.shape[0]
    own = lax.dynamic_slice_in_dim(base, start, count, axis=0).astype(jnp.float32)
    own_switch = lax.dynamic_slice_in_dim(switch, start, count, axis=0)
    return gather_rows((own + own_switch * total).astype(jnp.bfloat16), bits)


def shards(hidden_in, run_table, qkv_weight, out_weight, gate_up_weight, down_weight):
    tensor_parallel_count = lax.axis_size("tp")
    var_count = lax.axis_size("var")
    seq_count, full_len, model_width = hidden_in.shape
    row_count = seq_count * full_len
    query_slice = QUERY_HEADS // tensor_parallel_count
    key_value_slice = KEY_VALUE_HEADS // tensor_parallel_count
    group_width = QUERY_HEADS // KEY_VALUE_HEADS
    switches = run_table.astype(jnp.float32)
    bf16 = jnp.bfloat16

    block = down_weight.shape[1]
    half_block = block // 2
    ff_local = gate_up_weight.shape[2]
    qkv_full = gather(qkv_weight, 0)
    out_full = gather(out_weight, 1, qkv_full)

    columns = rms_norm(hidden_in).reshape(row_count, model_width)
    projected = jnp.dot(columns, qkv_full, preferred_element_type=jnp.float32)
    projected = projected.reshape(seq_count, full_len, query_slice + 2 * key_value_slice, HEAD_SIZE)
    queries, keys_values = projected[:, :, :query_slice], projected[:, :, query_slice:]
    token_positions = jnp.arange(full_len, dtype=jnp.float32)
    query_rows = rotary_embedding(queries, token_positions).astype(bf16)
    query_rows = query_rows.reshape(seq_count, full_len, key_value_slice, group_width, HEAD_SIZE)
    keys_bfloat = rotary_embedding(keys_values[:, :, :key_value_slice], token_positions).astype(bf16)
    values_bfloat = keys_values[:, :, key_value_slice:].astype(bf16)
    head_outputs = attend(query_rows, keys_bfloat, values_bfloat, HEAD_SIZE ** (-0.5))
    head_rows = head_outputs.reshape(row_count, query_slice * HEAD_SIZE)
    gate_up_full = gather(gate_up_weight.reshape(-1, 2 * ff_local), 0, out_full, head_rows)
    attn_terms = jnp.dot(head_rows, out_full, preferred_element_type=jnp.float32).astype(bf16)
    attn_switch = jnp.repeat(switches[:, 0], full_len)[:, None]
    flat_in = hidden_in.reshape(row_count, model_width)
    forth = list(range(tensor_parallel_count.bit_length() - 1))
    half_width = model_width // 2
    whole_after = jnp.concatenate(
        [
            add_sum(attn_terms[:, :half_width], flat_in[:, :half_width], attn_switch, forth),
            add_sum(attn_terms[:, half_width:], flat_in[:, half_width:], attn_switch, forth[::-1]),
        ],
        axis=1,
    )

    mlp_input = rms_norm(whole_after)
    down_a_full = gather(down_weight[:, :half_block], 1, gate_up_full, mlp_input)
    gate_and_up = jnp.dot(mlp_input, gate_up_full, preferred_element_type=jnp.float32)
    hidden = (jax.nn.silu(gate_and_up[:, :ff_local]) * gate_and_up[:, ff_local:]).astype(bf16)
    down_b_full = gather(down_weight[:, half_block:], 1, down_a_full, hidden)

    mlp_switch = jnp.repeat(switches[:, 1], full_len)[:, None]
    half_rows = row_count // 2
    results = []
    for number, down_full in enumerate((down_a_full, down_b_full)):
        if results:
            down_full = after(down_full, results[0])
        terms = jnp.dot(hidden, down_full, preferred_element_type=jnp.float32).astype(bf16)
        places = [var * block + number * half_block for var in range(var_count)]
        base = jnp.concatenate([whole_after[:, at : at + half_block] for at in places], axis=1)
        result = [
            add_sum(terms[:half_rows], base[:half_rows], mlp_switch[:half_rows], forth),
            add_sum(terms[half_rows:], base[half_rows:], mlp_switch[half_rows:], forth[::-1]),
        ]
        results.append(jnp.concatenate(result, axis=0))
    layer_out = jnp.concatenate(
        [
            result[:, at : at + half_block]
            for at in range(0, var_count * half_block, half_block)
            for result in results
        ],
        axis=1,
    )
    return layer_out.reshape(seq_count, full_len, model_width)


def solution(mesh):
    return jax.shard_map(
        shards,
        mesh=mesh,
        in_specs=(
            P("var", None, None),
            P("var", None),
            P("var", "tp"),
            P("tp", "var"),
            P("var", None, "tp"),
            P("tp", "var"),
        ),
        out_specs=P("var", None, None),
        check_vma=False,
    )
```

```python
import jax
import jax.numpy as jnp
from jax import lax
from jax.sharding import PartitionSpec as P

QUERY_HEADS = 32
KEY_VALUE_HEADS = 8
HEAD_SIZE = 64
CORES = 2


def rms_norm(tensor):
    widened = tensor.astype(jnp.float32)
    scaled = widened * lax.rsqrt(jnp.mean(widened * widened, axis=-1, keepdims=True) + 1e-05)
    return scaled.astype(jnp.bfloat16)


def rotary_embedding(tensor, token_positions):
    half_width = tensor.shape[-1] // 2
    exponent = jnp.arange(half_width, dtype=jnp.float32) * (2.0 / tensor.shape[-1])
    frequency = jnp.power(jnp.float32(500000.0), -exponent)
    angles = token_positions[:, None, None] * frequency[None, None, :]
    cosine = jnp.cos(angles)
    sine_part = jnp.sin(angles)
    first_half = tensor[..., :half_width]
    second_half = tensor[..., half_width:]
    return jnp.concatenate(
        [
            first_half * cosine - second_half * sine_part,
            second_half * cosine + first_half * sine_part,
        ],
        axis=-1,
    )


def attend(query_rows, keys_bfloat, values_bfloat, score_scale):
    scores = (
        jnp.einsum("bqkgd,bpkd->bkgqp", query_rows, keys_bfloat, preferred_element_type=jnp.float32)
        * score_scale
    )
    length = scores.shape[-1]
    causal = jnp.arange(length)[:, None] >= jnp.arange(length)[None, :]
    scores = jnp.where(causal, scores, jnp.float32(-1e30))
    row_max = jnp.max(scores, axis=-1, keepdims=True)
    exped = jnp.exp(scores - row_max)
    weights_bf = (exped / jnp.sum(exped, axis=-1, keepdims=True)).astype(jnp.bfloat16)
    head_outputs = jnp.einsum(
        "bkgqp,bpkd->bqkgd", weights_bf, values_bfloat, preferred_element_type=jnp.float32
    )
    return head_outputs.astype(jnp.bfloat16)


def after(tensor, earlier):
    return lax.optimization_barrier((tensor, earlier))[0]


def gather(shard, axis, *earlier):
    shard = after(shard, earlier) if earlier else shard
    return lax.all_gather(shard, "var", axis=axis, tiled=True)


def ring(shard, gates):
    var_count = lax.axis_size("var")
    forward = [(i, (i + CORES) % var_count) for i in range(var_count)]
    held = [shard]
    for hop in range(var_count // CORES - 1):
        sent = after(held[-1], gates[min(hop, len(gates) - 1)])
        held.append(lax.ppermute(sent, "var", forward))
    return held


def assemble_columns(held):
    var_count = lax.axis_size("var")
    chip_count = var_count // CORES
    pairs = [(i, i + 1 - 2 * (i % CORES)) for i in range(var_count)]
    me = lax.axis_index("var")
    chip, core = me // CORES, me % CORES
    rows, block = held[0].shape
    whole = jnp.zeros((rows, block * var_count), held[0].dtype)
    for step, shard in enumerate(held):
        other = lax.ppermute(shard, "var", pairs)
        pair = jnp.concatenate(
            [jnp.where(core == 0, shard, other), jnp.where(core == 0, other, shard)], axis=1
        )
        origin = (chip + chip_count - step) % chip_count
        whole = lax.dynamic_update_slice_in_dim(whole, pair, origin * CORES * block, axis=1)
    return whole


def partner(tensor, bit):
    pairs = [(i, i ^ (1 << bit)) for i in range(lax.axis_size("tp"))]
    return lax.ppermute(tensor, "tp", pairs)


def side(bit):
    return (lax.axis_index("tp") >> bit) & 1


def scatter_rows(terms, bits):
    start = 0
    for bit in bits:
        half = terms.shape[0] // 2
        mine = side(bit)
        sent = lax.dynamic_slice_in_dim(terms, (1 - mine) * half, half, axis=0)
        kept = lax.dynamic_slice_in_dim(terms, mine * half, half, axis=0)
        total = kept.astype(jnp.float32) + partner(sent, bit).astype(jnp.float32)
        terms = total.astype(jnp.bfloat16)
        start = start + mine * half
    return total, start


def gather_rows(rows, bits):
    for bit in bits[::-1]:
        other = partner(rows, bit)
        lower = side(bit) == 0
        rows = jnp.concatenate([jnp.where(lower, rows, other), jnp.where(lower, other, rows)], axis=0)
    return rows


def add_sum(terms, base, switch, bits):
    total, start = scatter_rows(terms, bits)
    count = total.shape[0]
    own = lax.dynamic_slice_in_dim(base, start, count, axis=0).astype(jnp.float32)
    own_switch = lax.dynamic_slice_in_dim(switch, start, count, axis=0)
    return gather_rows((own + own_switch * total).astype(jnp.bfloat16), bits)


def shards(hidden_in, run_table, qkv_weight, out_weight, gate_up_weight, down_weight):
    tensor_parallel_count = lax.axis_size("tp")
    var_count = lax.axis_size("var")
    seq_count, full_len, model_width = hidden_in.shape
    row_count = seq_count * full_len
    query_slice = QUERY_HEADS // tensor_parallel_count
    key_value_slice = KEY_VALUE_HEADS // tensor_parallel_count
    group_width = QUERY_HEADS // KEY_VALUE_HEADS
    switches = run_table.astype(jnp.float32)
    bf16 = jnp.bfloat16

    block = down_weight.shape[1]
    half_block = block // 2
    ff_local = gate_up_weight.shape[2]
    qkv_full = gather(qkv_weight, 0)
    out_full = gather(out_weight, 1, qkv_full)

    columns = rms_norm(hidden_in).reshape(row_count, model_width)
    projected = jnp.dot(columns, qkv_full, preferred_element_type=jnp.float32)
    projected = projected.reshape(seq_count, full_len, query_slice + 2 * key_value_slice, HEAD_SIZE)
    queries, keys_values = projected[:, :, :query_slice], projected[:, :, query_slice:]
    token_positions = jnp.arange(full_len, dtype=jnp.float32)
    query_rows = rotary_embedding(queries, token_positions).astype(bf16)
    query_rows = query_rows.reshape(seq_count, full_len, key_value_slice, group_width, HEAD_SIZE)
    keys_bfloat = rotary_embedding(keys_values[:, :, :key_value_slice], token_positions).astype(bf16)
    values_bfloat = keys_values[:, :, key_value_slice:].astype(bf16)
    head_outputs = attend(query_rows, keys_bfloat, values_bfloat, HEAD_SIZE ** (-0.5))
    head_rows = head_outputs.reshape(row_count, query_slice * HEAD_SIZE)
    gate_up_full = gather(gate_up_weight.reshape(-1, 2 * ff_local), 0, out_full, head_rows)
    attn_terms = jnp.dot(head_rows, out_full, preferred_element_type=jnp.float32).astype(bf16)
    attn_switch = jnp.repeat(switches[:, 0], full_len)[:, None]
    flat_in = hidden_in.reshape(row_count, model_width)
    forth = list(range(tensor_parallel_count.bit_length() - 1))
    half_width = model_width // 2
    whole_after = jnp.concatenate(
        [
            add_sum(attn_terms[:, :half_width], flat_in[:, :half_width], attn_switch, forth),
            add_sum(attn_terms[:, half_width:], flat_in[:, half_width:], attn_switch, forth[::-1]),
        ],
        axis=1,
    )

    mlp_input = rms_norm(whole_after)
    down_a_ring = ring(down_weight[:, :half_block], (qkv_full, head_rows, whole_after))
    down_a_full = assemble_columns(down_a_ring)
    down_b_full = gather(down_weight[:, half_block:], 1, gate_up_full, mlp_input, down_a_ring[-1])
    gate_and_up = jnp.dot(mlp_input, gate_up_full, preferred_element_type=jnp.float32)
    hidden = (jax.nn.silu(gate_and_up[:, :ff_local]) * gate_and_up[:, ff_local:]).astype(bf16)

    mlp_switch = jnp.repeat(switches[:, 1], full_len)[:, None]
    half_rows = row_count // 2
    results = []
    for number, down_full in enumerate((down_a_full, down_b_full)):
        terms = jnp.dot(hidden, down_full, preferred_element_type=jnp.float32).astype(bf16)
        places = [var * block + number * half_block for var in range(var_count)]
        base = jnp.concatenate([whole_after[:, at : at + half_block] for at in places], axis=1)
        result = [
            add_sum(terms[:half_rows], base[:half_rows], mlp_switch[:half_rows], forth),
            add_sum(terms[half_rows:], base[half_rows:], mlp_switch[half_rows:], forth[::-1]),
        ]
        results.append(jnp.concatenate(result, axis=0))
    layer_out = jnp.concatenate(
        [
            result[:, at : at + half_block]
            for at in range(0, var_count * half_block, half_block)
            for result in results
        ],
        axis=1,
    )
    return layer_out.reshape(seq_count, full_len, model_width)


def solution(mesh):
    return jax.shard_map(
        shards,
        mesh=mesh,
        in_specs=(
            P("var", None, None),
            P("var", None),
            P("var", "tp"),
            P("tp", "var"),
            P("var", None, "tp"),
            P("tp", "var"),
        ),
        out_specs=P("var", None, None),
        check_vma=False,
    )
```
